32 devices in a mesh: groups: 2 (over x), blk: 16 (over z, y, core).
Axes of the slice: x: 2, y: 2, z: 4, core: 2. Of those that a mesh axis runs over, the one named last changes fastest.
Arguments:
- queries: bfloat16 [24576, 1536], P(('groups', 'blk')), parts along dimension 0, may hold values from -20 to 20
- keys: bfloat16 [24576, 1536], P(('groups', 'blk')), parts along dimension 0, may hold values from -6 to 6
- values: bfloat16 [24576, 1536], P(('groups', 'blk')), parts along dimension 0, may hold values from -6 to 6
- neighbours: int32 [64, 7], P(('groups', 'blk')), parts along dimension 0, may hold values from -1 to 31, as said below
Outputs:
- attended: bfloat16 [24576, 1536], P(('groups', 'blk')), parts along dimension 0
The draws below stay inside these ranges and needn't reach their ends.
There are 2 independent parts, one for each index of `groups`. The reference program is written for one: setup_inputs(seed, part) draws one part's arguments, and reference() takes and returns one part's arrays. A program takes and returns all parts, laid end to end along the dimension named above; each array names one. Nothing has to cross between parts.
Inputs may be any that keep to these rules, and one draw needn't show every extreme that they name: `neighbours`: entry 0 of row t is t itself. Every other non-negative entry names a distinct tile of a frame block at most two blocks away from tile t's block; a slot is -1 only where its drawn tile falls outside the clip.
All inputs are finite; a program needn't handle non-finite values.
Results may differ from the reference program's by a relative error of at most 0.0048.
Values may be sent and summed in bfloat16 or wider, within the bound.
No kernel may reach another device: no remote copies, remote signals or barrier semaphores. Data moves between devices by JAX's collectives and lax.ppermute only.
A program may use at most 128 MiB of HBM per device.

```python
import jax
import jax.numpy as jnp
from jax import lax

HEADS = 12
HD = 128
TILE = 384
NBR = 7
TILES_DEV = 2
TILES = 32
TOKENS = 12288


def query_key_pair(key):
    query_key = jax.random.fold_in(key, 11)
    key_key = jax.random.fold_in(key, 12)
    shape = (TOKENS, HEADS * HD)
    keys_drawn = jnp.clip(jax.random.normal(key_key, shape, jnp.float32), -6.0, 6.0)
    queries_drawn = jnp.clip(jax.random.normal(query_key, shape, jnp.float32), -6.0, 6.0)
    return (queries_drawn, keys_drawn)


def draw_queries(key, part):
    return query_key_pair(key)[0].astype(jnp.bfloat16)


def draw_keys(key, part):
    return query_key_pair(key)[1].astype(jnp.bfloat16)


def draw_neighbours(key, part):
    candidates = 5 * TILES_DEV
    rows = jnp.arange(TILES, dtype=jnp.int32)
    block = rows // TILES_DEV
    base = (block - 2) * TILES_DEV
    own_offset = rows - base
    row_keys = jax.random.split(jax.random.fold_in(key, 21), TILES)
    picks = jax.vmap(lambda row_key: jax.random.permutation(row_key, candidates - 1))(row_keys)[:, :NBR - 1]
    offsets = picks + (picks >= own_offset[:, None]).astype(jnp.int32)
    others = base[:, None] + offsets
    others = jnp.where((others >= 0) & (others < TILES), others, -1)
    return jnp.concatenate([rows[:, None], others], axis=1).astype(jnp.int32)


def level_of(own_key, extent, cuts, low, largest):
    def one(dim, parts):
        steps = jax.random.uniform(jax.random.fold_in(jax.random.fold_in(own_key, 6), dim), (parts,), jnp.float32, low / len(cuts), largest / len(cuts))
        return jnp.repeat(jnp.exp(steps), extent[dim] // parts).reshape((-1,) + (1,) * (len(extent) - dim - 1))

    loudness = one(*cuts[0])
    for cut in cuts[1:]:
        loudness = loudness * one(*cut)
    return loudness


def scatter_about(stream_key, extent, deviation, most, cuts=(), kind=jnp.bfloat16):
    loudness = level_of(stream_key, extent, cuts, -0.22, 0.18) if cuts else 1.0
    array = jax.random.normal(stream_key, extent, jnp.float32) * deviation * loudness
    return jnp.minimum(jnp.maximum(array, -most), most).astype(kind)


def setup_inputs(seed: int = 0, part: int = 0) -> dict:
    arg_keys = jax.random.split(jax.random.key(seed), 5)
    part_splits = jax.random.split(jax.random.fold_in(arg_keys[4], part), 5)
    return {
        "queries": draw_queries(jax.random.fold_in(jax.random.fold_in(arg_keys[4], part), 71), part),
        "keys": draw_keys(jax.random.fold_in(jax.random.fold_in(arg_keys[4], part), 71), part),
        "values": scatter_about(part_splits[2], (TOKENS, HEADS * HD), 1.0, 6.0, ((0, 16),)),
        "neighbours": draw_neighbours(jax.random.fold_in(jax.random.fold_in(arg_keys[4], part), 71), part),
    }


def reference(queries, keys, values, neighbours):
    scale = HD ** -0.5
    q_tiles = queries.reshape(TILES, TILE, HEADS, HD)
    k_tiles = keys.reshape(TILES, TILE, HEADS, HD)
    v_tiles = values.reshape(TILES, TILE, HEADS, HD)

    def one_tile(tile_id):
        named = neighbours[tile_id]
        valid = named >= 0
        safe = jnp.where(valid, named, 0).astype(jnp.int32)
        key_rows = k_tiles[safe].reshape(NBR * TILE, HEADS, HD).astype(jnp.float32)
        value_rows = v_tiles[safe].reshape(NBR * TILE, HEADS, HD).astype(jnp.float32)
        query_rows = q_tiles[tile_id].astype(jnp.float32)
        scores = jnp.einsum("qhd,khd->hqk", query_rows, key_rows) * scale
        key_mask = jnp.repeat(valid, TILE)
        scores = jnp.where(key_mask[None, None, :], scores, -jnp.inf)
        peak = jnp.max(scores, axis=2, keepdims=True)
        weights = jnp.exp(scores - peak)
        total = jnp.sum(weights, axis=2)
        rounded = lax.optimization_barrier(weights.astype(jnp.bfloat16)).astype(jnp.float32)
        summed = jnp.einsum("hqk,khd->qhd", rounded, value_rows)
        result = summed / jnp.transpose(total)[:, :, None]
        return result.astype(jnp.bfloat16).reshape(TILE, HEADS * HD)

    output = lax.map(one_tile, jnp.arange(TILES, dtype=jnp.int32))
    return output.reshape(TILES * TILE, HEADS * HD)
```

```python
import functools

import jax
import jax.numpy as jnp
from jax import lax
from jax.experimental import pallas as pl
from jax.experimental.pallas import tpu as pltpu
from jax.sharding import PartitionSpec as P

HD = 128
LOG2E = 1.4426950408889634
SOURCES = 6
HEAD_US = 6


def heads_kernel(
    heads, first, slots, tile, table, place, q_ref, k_own, v_own, k_mate, v_mate, *rest
):
    far = rest[:4]
    out_ref, k_win, v_win, scores, sems = rest[-5:]
    step = pl.program_id(0)
    rows, hd = q_ref.shape
    tiles = rows // tile

    def copies(at, slot):
        col = pl.ds(pl.multiple_of((first + at) * hd, hd), hd)
        k_col = pl.ds(pl.multiple_of(at * hd, hd), hd)
        v_col = pl.ds(pl.multiple_of((heads + at) * hd, hd), hd)
        pairs = [(k_own.at[:, col], v_own.at[:, col])]
        pairs += [(k_mate.at[:, col], v_mate.at[:, col])]
        pairs += [(block.at[:, k_col], block.at[:, v_col]) for block in far]
        made = []
        for source, (k, v) in enumerate(pairs):
            where = pl.ds(pl.multiple_of(place[source] * rows, rows), rows)
            made.append(pltpu.make_async_copy(k, k_win.at[slot, where], sems.at[slot, source, 0]))
            made.append(pltpu.make_async_copy(v, v_win.at[slot, where], sems.at[slot, source, 1]))
        return made

    slot = lax.rem(step, 2)

    @pl.when(step == 0)
    def _():
        for copy in copies(0, 0):
            copy.start()

    @pl.when(step + 1 < heads)
    def _():
        for copy in copies(step + 1, 1 - slot):
            copy.start()

    for copy in copies(step, slot):
        copy.wait()

    factor = hd**-0.5 * LOG2E
    for t in range(tiles):
        valid = []
        starts = []
        for j in range(slots):
            named = table[t * slots + j]
            valid.append(named >= 0)
            starts.append(pl.multiple_of(jnp.maximum(named, 0) * tile, tile))
        q = q_ref[t * tile : (t + 1) * tile, :]
        peak = None
        for j in range(slots):
            k = k_win[slot, pl.ds(starts[j], tile), :]
            s = lax.dot_general(
                q, k, (((1,), (1,)), ((), ())), preferred_element_type=jnp.float32
            )
            s = s * factor
            scores[j] = s
            most = s[:, :128]
            for lane in range(128, tile, 128):
                most = jnp.maximum(most, s[:, lane : lane + 128])
            most = jnp.where(valid[j], most, -3e38)
            peak = most if peak is None else jnp.maximum(peak, most)
        peak = jnp.max(peak, axis=1, keepdims=True)
        total = None
        summed = None
        for j in range(slots):
            weights = jnp.exp2(scores[j] - jnp.where(valid[j], peak, 3e38))
            part = weights[:, :128]
            for lane in range(128, tile, 128):
                part = part + weights[:, lane : lane + 128]
            total = part if total is None else total + part
            v = v_win[slot, pl.ds(starts[j], tile), :]
            term = jnp.dot(weights.astype(jnp.bfloat16), v, preferred_element_type=jnp.float32)
            summed = term if summed is None else summed + term
        total = jnp.sum(total, axis=1, keepdims=True)
        out_ref[t * tile : (t + 1) * tile, :] = (summed / total).astype(out_ref.dtype)


def attend(first, heads, tile, table, place, queries, blocks, previous):
    rows, width = queries.shape
    slots = table.shape[0] // (rows // tile)
    anywhere = pl.BlockSpec(memory_space=pl.ANY)
    one_head = pl.BlockSpec((rows, HD), lambda step, *_: (0, first + step))
    operands = [table, place, queries, *blocks]
    specs = [one_head] + [anywhere] * len(blocks)
    aliases = {}
    if previous is not None:
        aliases = {len(operands): 0}
        operands.append(previous)
        specs.append(anywhere)
    return pl.pallas_call(
        functools.partial(heads_kernel, heads, first, slots, tile),
        out_shape=jax.ShapeDtypeStruct((rows, width), queries.dtype),
        grid_spec=pltpu.PrefetchScalarGridSpec(
            num_scalar_prefetch=2,
            grid=(heads,),
            in_specs=specs,
            out_specs=one_head,
            scratch_shapes=[
                pltpu.VMEM((2, SOURCES * rows, HD), queries.dtype),
                pltpu.VMEM((2, SOURCES * rows, HD), queries.dtype),
                pltpu.VMEM((slots, tile, tile), jnp.float32),
                pltpu.SemaphoreType.DMA((2, SOURCES, 2)),
            ],
        ),
        input_output_aliases=aliases,
        compiler_params=pltpu.CompilerParams(vmem_limit_bytes=40 * 1024 * 1024),
        cost_estimate=pl.CostEstimate(
            flops=4 * heads * rows * slots * tile * HD,
            bytes_accessed=heads * rows * HD * 2 * 14,
            transcendentals=heads * rows * slots * tile,
        ),
    )(*operands)


def head_cuts(head_count):
    return [2] * (head_count // 2) + [1] * (head_count % 2)


def on_device(queries, keys, values, neighbours):
    rows, width = queries.shape
    tiles = neighbours.shape[0]
    tile = rows // tiles
    count = lax.axis_size("blk")
    block = lax.axis_index("blk")
    cuts = head_cuts(width // HD)

    quads = range(0, count, 4)
    mates = [(b, b ^ 1) for b in range(count)]
    across = [(b, b ^ 2) for b in range(count)]
    onward = [(b, b + 4 if b % 4 < 2 else b - 4) for b in range(count)]
    onward = [(b, to) for b, to in onward if 0 <= to < count]
    pass_first = [pair for b in quads for pair in ((b, b + 1), (b + 3, b + 2))]
    pass_second = [pair for b in quads for pair in ((b + 1, b), (b + 2, b + 3))]

    place = jnp.array(
        [
            [2, 3, 4, 0, 5, 1],
            [2, 1, 4, 0, 3, 5],
            [2, 3, 0, 4, 1, 5],
            [2, 1, 0, 4, 5, 3],
        ],
        jnp.int32,
    )[lax.rem(block, 4)]
    base = (block - 2) * tiles
    table = jnp.where(neighbours >= 0, neighbours - base, -1).reshape(-1)

    k_mate = lax.ppermute(keys, "blk", mates)
    v_mate = lax.ppermute(values, "blk", mates)

    output = None
    first = 0
    crossed = []
    waiting = []
    for chunk, heads in enumerate(cuts):
        cols = slice(first * HD, (first + heads) * HD)
        k_part, v_part = keys[:, cols], values[:, cols]
        if chunk >= 2:
            k_part, v_part, crossed[chunk - 2] = lax.optimization_barrier(
                (k_part, v_part, crossed[chunk - 2])
            )
        packed = jnp.concatenate([k_part, v_part], axis=1)
        crossed.append(lax.ppermute(packed, "blk", across))
        first += heads
    first = 0
    for chunk, heads in enumerate(cuts):
        y = crossed[chunk]
        z = lax.ppermute(y, "blk", onward)
        y_pass = lax.ppermute(y, "blk", pass_first)
        z_pass = lax.ppermute(z, "blk", pass_second)
        blocks = (keys, values, k_mate, v_mate, y, z, y_pass, z_pass)
        output = attend(first, heads, tile, table, place, queries, blocks, output)
        first += heads
    return output


def solution(mesh):
    spec = P(("groups", "blk"), None)
    return jax.shard_map(
        on_device, mesh=mesh, in_specs=(spec,) * 4, out_specs=spec, check_vma=False
    )
```

```python
import functools

import jax
import jax.numpy as jnp
from jax import lax
from jax.experimental import pallas as pl
from jax.experimental.pallas import tpu as pltpu
from jax.sharding import PartitionSpec as P

HD = 128
LOG2E = 1.4426950408889634
AHEAD = 2
VMEM_BYTES = 56 * 2**20
SOURCES = 6
SMALL = pl.CostEstimate(flops=1, bytes_accessed=1, transcendentals=0)
HBM = pl.BlockSpec(memory_space=pltpu.HBM)


def lanes(start, size):
    return pl.ds(pl.multiple_of(start, HD), size)


def run_copies(pairs, sems):
    made = [pltpu.make_async_copy(a, b, sems.at[i]) for i, (a, b) in enumerate(pairs)]
    for copy in made:
        copy.start()
    return made


def pack(plan, core, operands, shapes, most):
    count = len(operands)
    made = len(shapes)
    kind = operands[0].dtype

    def body(core_ref, *refs):
        outs = refs[count : count + made]
        held = refs[count + made : -2]
        in_sems, out_sems = refs[-2:]
        loads = [
            run_copies(pairs, in_sems.at[i])
            for i, pairs in enumerate(plan(core_ref[0], refs[:count], held))
        ]
        stores = []
        for i, load in enumerate(loads):
            for copy in load:
                copy.wait()
            stores += run_copies([(held[i], outs[i])], out_sems.at[pl.ds(i, 1)])
        for copy in stores:
            copy.wait()

    return pl.pallas_call(
        body,
        out_shape=[jax.ShapeDtypeStruct(shape, kind) for shape in shapes],
        in_specs=[pl.BlockSpec(memory_space=pltpu.SMEM)] + [HBM] * count,
        out_specs=[HBM] * made,
        scratch_shapes=[pltpu.VMEM(shape, kind) for shape in shapes]
        + [pltpu.SemaphoreType.DMA((made, most)), pltpu.SemaphoreType.DMA((made,))],
        compiler_params=pltpu.CompilerParams(vmem_limit_bytes=VMEM_BYTES),
        cost_estimate=SMALL,
    )(core, *operands)


def head_kernel(sides, head, half, to_col, slots, tile, table, place, *refs):
    queries, m_q = refs[:2]
    blocks = refs[2 : 2 + SOURCES]
    outs = refs[-8 - len(sides) : -8]
    q_win, k_win, v_win, o_win, s_even, s_odd, sems, out_sems = refs[-8:]
    rows = queries.shape[0]
    col = lanes((place[SOURCES] * half + head) * HD, HD)
    q_from = (queries.at[:, col], m_q.at[:, pl.ds(head * HD, HD)])
    where = [pl.ds(pl.multiple_of(place[s] * rows, rows), rows) for s in range(SOURCES)]
    loads = [(q_from[side], q_win.at[pl.ds(i * rows, rows)]) for i, side in enumerate(sides)]
    loads += [(block.at[pl.ds(0, rows)], k_win.at[w]) for block, w in zip(blocks, where)]
    loads += [(block.at[pl.ds(rows, rows)], v_win.at[w]) for block, w in zip(blocks, where)]
    loads = run_copies(loads, sems)
    for copy in loads[:-SOURCES]:
        copy.wait()

    factor = HD**-0.5 * LOG2E
    scores = (s_even, s_odd)
    part = s_even.shape[1]
    tiles = rows // tile
    units = [(t, r) for t in range(len(sides) * tiles) for r in range(0, tile, part)]
    peaks = {}
    stores = []

    def named(t, j):
        at = table[(sides[t // tiles] * tiles + t % tiles) * slots + j]
        return at >= 0, pl.ds(pl.multiple_of(jnp.maximum(at, 0) * tile, tile), tile)

    for u in range(len(units) + 1):
        peak = total = summed = None
        if u == 1:
            for copy in loads[-SOURCES:]:
                copy.wait()
        for j in range(slots):
            if u < len(units):
                t, r = units[u]
                valid, at = named(t, j)
                s = lax.dot_general(
                    q_win[t * tile + r : t * tile + r + part, :],
                    k_win[at, :],
                    (((1,), (1,)), ((), ())),
                    preferred_element_type=jnp.float32,
                )
                s = s * factor
                scores[u % 2][j] = s
                most = s[:, :HD]
                for lane in range(HD, tile, HD):
                    most = jnp.maximum(most, s[:, lane : lane + HD])
                most = jnp.where(valid, most, -3e38)
                peak = most if peak is None else jnp.maximum(peak, most)
            if u > 0:
                valid, at = named(units[u - 1][0], j)
                above = jnp.where(valid, peaks[u - 1], 3e38)
                weights = jnp.exp2(scores[(u - 1) % 2][j] - above)
                added = weights[:, :HD]
                for lane in range(HD, tile, HD):
                    added = added + weights[:, lane : lane + HD]
                total = added if total is None else total + added
                term = jnp.dot(
                    weights.astype(jnp.bfloat16),
                    v_win[at, :],
                    preferred_element_type=jnp.float32,
                )
                summed = term if summed is None else summed + term
        if u < len(units):
            peaks[u] = jnp.max(peak, axis=1, keepdims=True)
        if u > 0:
            t, r = units[u - 1]
            result = summed / jnp.sum(total, axis=1, keepdims=True)
            o_win[t * tile + r : t * tile + r + part, :] = result.astype(o_win.dtype)
            if t % tiles == tiles - 1 and r + part == tile:
                i = t // tiles
                to = col if sides[i] == 0 else pl.ds(to_col * HD, HD)
                pair = (o_win.at[pl.ds(i * rows, rows)], outs[i].at[:, to])
                stores += run_copies([pair], out_sems.at[pl.ds(i, 1)])
    for copy in stores:
        copy.wait()


def attend(sides, head, half, to_col, part, tile, table, place, operands, previous, widths):
    rows = operands[0].shape[0]
    slots = table.shape[0] // (2 * (rows // tile))
    kind = operands[0].dtype
    smem = pl.BlockSpec(memory_space=pltpu.SMEM)
    ins = [table, place, *operands]
    aliases = {}
    for i, array in enumerate(previous):
        if array is not None:
            aliases[len(ins)] = i
            ins.append(array)
    count = len(sides)
    return pl.pallas_call(
        functools.partial(head_kernel, sides, head, half, to_col, slots, tile),
        out_shape=[jax.ShapeDtypeStruct((rows, width), kind) for width in widths],
        in_specs=[smem] * 2 + [HBM] * (len(ins) - 2),
        out_specs=[HBM] * count,
        scratch_shapes=[
            pltpu.VMEM((count * rows, HD), kind),
            pltpu.VMEM((SOURCES * rows, HD), kind),
            pltpu.VMEM((SOURCES * rows, HD), kind),
            pltpu.VMEM((count * rows, HD), kind),
            pltpu.VMEM((slots, part, tile), jnp.float32),
            pltpu.VMEM((slots, part, tile), jnp.float32),
            pltpu.SemaphoreType.DMA((count + 2 * SOURCES,)),
            pltpu.SemaphoreType.DMA((count,)),
        ],
        input_output_aliases=aliases,
        compiler_params=pltpu.CompilerParams(vmem_limit_bytes=VMEM_BYTES),
        cost_estimate=SMALL,
    )(*ins)


def on_device(queries, keys, values, neighbours):
    rows, width = queries.shape
    tiles = neighbours.shape[0]
    tile = rows // tiles
    count = lax.axis_size("blk")
    block = lax.axis_index("blk")
    half = width // HD // 2
    hw = half * HD
    core = lax.rem(block, 2)
    upper = lax.rem(block // 2, 2)

    mates = [(b, b ^ 1) for b in range(count)]
    across = [(b, b ^ 2) for b in range(count)]
    onward = [(b, (b + 4 if b % 4 < 2 else b - 4) % count) for b in range(count)]

    def move(value, pairs):
        return lax.ppermute(value, "blk", pairs)

    crossed_at = 4 * (1 - upper)
    place = jnp.stack(
        [
            2 + core,
            3 - core,
            crossed_at + core,
            crossed_at + 1 - core,
            4 - crossed_at + core,
            5 - crossed_at - core,
            core,
        ]
    ).astype(jnp.int32)
    core_id = core.astype(jnp.int32).reshape(1)

    order = [(0, 0), (0, 1), (1, 0), (1, 1)]
    order += [(side, h) for h in range(2, half) for side in (0, 1)]

    def cut(refs, head, out):
        col = lanes(head * HD, HD)
        return [(refs[i].at[:, col], out.at[pl.ds(i * rows, rows)]) for i in range(2)]

    def plan_first(k, refs, outs):
        plans = [cut(refs, k * half + h, outs[h]) for h in range(2)]
        for h in range(half):
            to = outs[2].at[pl.ds(2 * h * rows, 2 * rows)]
            plans.append(cut(refs, (1 - k) * half + h, to))
        return plans[:2] + [sum(plans[2:], [])]

    def plan_second(k, refs, outs):
        plans = [[(refs[3].at[pl.ds(2 * h * rows, 2 * rows)], outs[h])] for h in range(half)]
        plans += [cut(refs, k * half + h, outs[half + h - 2]) for h in range(2, half)]
        return plans + [[(refs[2].at[:, lanes((1 - k) * hw, hw)], outs[-1])]]

    def after(value, *earlier):
        return lax.optimization_barrier((value, earlier))[0]

    piece = (2 * rows, HD)
    pieces = {}
    crossed = []
    pieces[0, 0], pieces[0, 1], theirs = pack(
        plan_first, core_id, (keys, values), [piece] * 2 + [(2 * half * rows, HD)], 2 * half
    )
    m_kv = move(theirs, mates)
    for h in range(2):
        crossed.append(move(pieces[0, h], across))
    second = pack(
        plan_second,
        core_id,
        (*after((keys, values, queries), crossed[0]), m_kv),
        [piece] * (2 * half - 2) + [(rows, hw)],
        2,
    )
    for h in range(half):
        pieces[1, h] = second[h]
        if h >= 2:
            pieces[0, h] = second[half + h - 2]
    m_q = move(second[-1], mates)
    base = (block - core - 2) * tiles
    listed = jnp.concatenate([neighbours, move(neighbours, mates)], axis=0)
    table = jnp.where(listed >= 0, listed - base, -1).reshape(-1).astype(jnp.int32)
    order = [(0, 0), (0, 1), (1, 0), (1, 1)]
    order += [(side, h) for h in range(2, half) for side in (0, 1)]
    for i, entry in enumerate(order):
        if i < 2:
            continue
        going = pieces[entry]
        if i >= AHEAD:
            going = after(going, crossed[i - AHEAD])
        if i == 5:
            going = after(going, m_q)
        crossed.append(move(going, across))

    spot = {entry: i for i, entry in enumerate(order)}
    came = []
    output = None
    passed = None
    last_passed = None

    def compute(sides, h, *earlier):
        nonlocal output, passed, last_passed
        pair = [spot[(0, h)], spot[(1, h)]]
        operands = [queries, m_q, pieces[0, h], pieces[1, h]]
        for held in (crossed, came):
            operands += [held[at] for at in pair]
        if earlier:
            operands = after(operands, *earlier)
        fixed = (table, place, operands)
        part = tile if len(sides) == 2 else tile // 2
        if sides == (0,):
            (output,) = attend(sides, h, half, 0, part, tile, *fixed, [output], [width])
        elif sides == (1,):
            (last_passed,) = attend(sides, h, half, 0, part, tile, *fixed, [None], [HD])
        else:
            output, passed = attend(
                sides, h, half, h, part, tile, *fixed, [output, passed], [width, hw - HD]
            )

    for i in range(len(order)):
        going = crossed[i]
        if i >= 2:
            going = after(going, came[i - 2])
        if output is not None:
            going = after(going, output)
        came.append(move(going, onward))
        if i >= 3 and i % 2 == 1:
            compute((0, 1), (i - 3) // 2)
    compute((1,), half - 1)
    compute((0,), half - 1)

    back = move(after(passed, last_passed), mates)
    last_back = move(last_passed, mates)

    def finish(core_ref, back_ref, last_ref, _, out_ref, held, sems):
        loads = run_copies(
            [(back_ref, held.at[:, pl.ds(0, hw - HD)]), (last_ref, held.at[:, pl.ds(hw - HD, HD)])],
            sems,
        )
        for copy in loads:
            copy.wait()
        column = lanes((1 - core_ref[0]) * hw, hw)
        for copy in run_copies([(held, out_ref.at[:, column])], sems.at[pl.ds(2, 1)]):
            copy.wait()

    return pl.pallas_call(
        finish,
        out_shape=jax.ShapeDtypeStruct((rows, width), queries.dtype),
        in_specs=[pl.BlockSpec(memory_space=pltpu.SMEM)] + [HBM] * 3,
        out_specs=HBM,
        scratch_shapes=[pltpu.VMEM((rows, hw), queries.dtype), pltpu.SemaphoreType.DMA((3,))],
        input_output_aliases={3: 0},
        compiler_params=pltpu.CompilerParams(vmem_limit_bytes=VMEM_BYTES),
    )(core_id, back, last_back, output)


def solution(mesh):
    spec = P(("groups", "blk"), None)
    return jax.shard_map(
        on_device, mesh=mesh, in_specs=(spec,) * 4, out_specs=spec, check_vma=False
    )
```

```python
import functools

import jax
import jax.numpy as jnp
from jax import lax
from jax.experimental import pallas as pl
from jax.experimental.pallas import tpu as pltpu
from jax.sharding import PartitionSpec as P

HD = 128
LOG2E = 1.4426950408889634
AHEAD = 2
VMEM_BYTES = 56 * 2**20
SOURCES = 6
SMALL = pl.CostEstimate(flops=1, bytes_accessed=1, transcendentals=0)
HBM = pl.BlockSpec(memory_space=pltpu.HBM)


def lanes(start, size):
    return pl.ds(pl.multiple_of(start, HD), size)


def run_copies(pairs, sems):
    made = [pltpu.make_async_copy(a, b, sems.at[i]) for i, (a, b) in enumerate(pairs)]
    for copy in made:
        copy.start()
    return made


def pack(plan, core, operands, shapes, most):
    count = len(operands)
    made = len(shapes)
    kind = operands[0].dtype

    def body(core_ref, *refs):
        outs = refs[count : count + made]
        held = refs[count + made : -2]
        in_sems, out_sems = refs[-2:]
        loads = [
            run_copies(pairs, in_sems.at[i])
            for i, pairs in enumerate(plan(core_ref[0], refs[:count], held))
        ]
        stores = []
        for i, load in enumerate(loads):
            for copy in load:
                copy.wait()
            stores += run_copies([(held[i], outs[i])], out_sems.at[pl.ds(i, 1)])
        for copy in stores:
            copy.wait()

    return pl.pallas_call(
        body,
        out_shape=[jax.ShapeDtypeStruct(shape, kind) for shape in shapes],
        in_specs=[pl.BlockSpec(memory_space=pltpu.SMEM)] + [HBM] * count,
        out_specs=[HBM] * made,
        scratch_shapes=[pltpu.VMEM(shape, kind) for shape in shapes]
        + [pltpu.SemaphoreType.DMA((made, most)), pltpu.SemaphoreType.DMA((made,))],
        compiler_params=pltpu.CompilerParams(vmem_limit_bytes=VMEM_BYTES),
        cost_estimate=SMALL,
    )(core, *operands)


def head_kernel(sides, head, half, to_col, slots, tile, table, place, *refs):
    queries, m_q = refs[:2]
    blocks = refs[2 : 2 + SOURCES]
    outs = refs[-8 - len(sides) : -8]
    q_win, k_win, v_win, o_win, s_even, s_odd, sems, out_sems = refs[-8:]
    rows = queries.shape[0]
    col = lanes((place[SOURCES] * half + head) * HD, HD)
    q_from = (queries.at[:, col], m_q.at[:, pl.ds(head * HD, HD)])
    where = [pl.ds(pl.multiple_of(place[s] * rows, rows), rows) for s in range(SOURCES)]
    loads = [(q_from[side], q_win.at[pl.ds(i * rows, rows)]) for i, side in enumerate(sides)]
    for i, window in enumerate((k_win, v_win)):
        for s, block in enumerate(blocks):
            at = pl.ds((2 * head + i if s == 1 else i) * rows, rows)
            loads.append((block.at[at], window.at[where[s]]))
    loads = run_copies(loads, sems)
    for copy in loads[:-SOURCES]:
        copy.wait()

    factor = HD**-0.5 * LOG2E
    scores = (s_even, s_odd)
    part = s_even.shape[1]
    tiles = rows // tile
    units = [(t, r) for t in range(len(sides) * tiles) for r in range(0, tile, part)]
    peaks = {}
    stores = []

    def named(t, j):
        at = table[(sides[t // tiles] * tiles + t % tiles) * slots + j]
        return at >= 0, pl.ds(pl.multiple_of(jnp.maximum(at, 0) * tile, tile), tile)

    for u in range(len(units) + 1):
        peak = total = summed = None
        if u == 1:
            for copy in loads[-SOURCES:]:
                copy.wait()
        for j in range(slots):
            if u < len(units):
                t, r = units[u]
                valid, at = named(t, j)
                s = lax.dot_general(
                    q_win[t * tile + r : t * tile + r + part, :],
                    k_win[at, :],
                    (((1,), (1,)), ((), ())),
                    preferred_element_type=jnp.float32,
                )
                s = s * factor
                scores[u % 2][j] = s
                most = s[:, :HD]
                for lane in range(HD, tile, HD):
                    most = jnp.maximum(most, s[:, lane : lane + HD])
                most = jnp.where(valid, most, -3e38)
                peak = most if peak is None else jnp.maximum(peak, most)
            if u > 0:
                valid, at = named(units[u - 1][0], j)
                above = jnp.where(valid, peaks[u - 1], 3e38)
                weights = jnp.exp2(scores[(u - 1) % 2][j] - above)
                added = weights[:, :HD]
                for lane in range(HD, tile, HD):
                    added = added + weights[:, lane : lane + HD]
                total = added if total is None else total + added
                term = jnp.dot(
                    weights.astype(jnp.bfloat16),
                    v_win[at, :],
                    preferred_element_type=jnp.float32,
                )
                summed = term if summed is None else summed + term
        if u < len(units):
            peaks[u] = jnp.max(peak, axis=1, keepdims=True)
        if u > 0:
            t, r = units[u - 1]
            result = summed / jnp.sum(total, axis=1, keepdims=True)
            o_win[t * tile + r : t * tile + r + part, :] = result.astype(o_win.dtype)
            if t % tiles == tiles - 1 and r + part == tile:
                i = t // tiles
                to = col if sides[i] == 0 else pl.ds(to_col * HD, HD)
                pair = (o_win.at[pl.ds(i * rows, rows)], outs[i].at[:, to])
                stores += run_copies([pair], out_sems.at[pl.ds(i, 1)])
    for copy in stores:
        copy.wait()


def attend(sides, head, half, to_col, part, tile, table, place, operands, previous, widths):
    rows = operands[0].shape[0]
    slots = table.shape[0] // (2 * (rows // tile))
    kind = operands[0].dtype
    smem = pl.BlockSpec(memory_space=pltpu.SMEM)
    ins = [table, place, *operands]
    aliases = {}
    for i, array in enumerate(previous):
        if array is not None:
            aliases[len(ins)] = i
            ins.append(array)
    count = len(sides)
    return pl.pallas_call(
        functools.partial(head_kernel, sides, head, half, to_col, slots, tile),
        out_shape=[jax.ShapeDtypeStruct((rows, width), kind) for width in widths],
        in_specs=[smem] * 2 + [HBM] * (len(ins) - 2),
        out_specs=[HBM] * count,
        scratch_shapes=[
            pltpu.VMEM((count * rows, HD), kind),
            pltpu.VMEM((SOURCES * rows, HD), kind),
            pltpu.VMEM((SOURCES * rows, HD), kind),
            pltpu.VMEM((count * rows, HD), kind),
            pltpu.VMEM((slots, part, tile), jnp.float32),
            pltpu.VMEM((slots, part, tile), jnp.float32),
            pltpu.SemaphoreType.DMA((count + 2 * SOURCES,)),
            pltpu.SemaphoreType.DMA((count,)),
        ],
        input_output_aliases=aliases,
        compiler_params=pltpu.CompilerParams(vmem_limit_bytes=VMEM_BYTES),
        cost_estimate=SMALL,
    )(*ins)


def on_device(queries, keys, values, neighbours):
    rows, width = queries.shape
    tiles = neighbours.shape[0]
    tile = rows // tiles
    count = lax.axis_size("blk")
    block = lax.axis_index("blk")
    half = width // HD // 2
    hw = half * HD
    core = lax.rem(block, 2)
    upper = lax.rem(block // 2, 2)

    mates = [(b, b ^ 1) for b in range(count)]
    across = [(b, b ^ 2) for b in range(count)]
    onward = [(b, (b + 4 if b % 4 < 2 else b - 4) % count) for b in range(count)]

    def move(value, pairs):
        return lax.ppermute(value, "blk", pairs)

    crossed_at = 4 * (1 - upper)
    place = jnp.stack(
        [
            2 + core,
            3 - core,
            crossed_at + core,
            crossed_at + 1 - core,
            4 - crossed_at + core,
            5 - crossed_at - core,
            core,
        ]
    ).astype(jnp.int32)
    core_id = core.astype(jnp.int32).reshape(1)


    def cut(refs, head, out):
        col = lanes(head * HD, HD)
        return [(refs[i].at[:, col], out.at[pl.ds(i * rows, rows)]) for i in range(2)]

    def plan(k, refs, outs):
        plans = [cut(refs, k * half + h, outs[h]) for h in range(half)]
        away = []
        for h in range(half):
            to = outs[half].at[pl.ds(2 * h * rows, 2 * rows)]
            away += cut(refs, (1 - k) * half + h, to)
        return plans + [away, [(refs[2].at[:, lanes((1 - k) * hw, hw)], outs[-1])]]

    def after(value, *earlier):
        return lax.optimization_barrier((value, earlier))[0]

    piece = (2 * rows, HD)
    crossed = []
    *own, kv_away, q_away = pack(
        plan,
        core_id,
        (keys, values, queries),
        [piece] * half + [(2 * half * rows, HD), (rows, hw)],
        2 * half,
    )
    m_kv = move(kv_away, mates)
    m_q = move(q_away, mates)
    base = (block - core - 2) * tiles
    listed = jnp.concatenate([neighbours, move(neighbours, mates)], axis=0)
    table = jnp.where(listed >= 0, listed - base, -1).reshape(-1).astype(jnp.int32)
    order = [(0, 0), (0, 1), (1, 0), (1, 1)]
    order += [(side, h) for h in range(2, half) for side in (0, 1)]
    for i, entry in enumerate(order):
        side, h = entry
        going = m_kv[2 * h * rows : 2 * (h + 1) * rows] if side else own[h]
        lag = 2 if i < 5 else 4
        if i >= lag:
            going = after(going, crossed[i - lag])
        crossed.append(move(going, across))

    spot = {entry: i for i, entry in enumerate(order)}
    came = []
    output = None
    passed = None

    def compute(sides, h, *earlier):
        nonlocal output, passed
        pair = [spot[(0, h)], spot[(1, h)]]
        operands = [queries, m_q, own[h], m_kv]
        for held in (crossed, came):
            operands += [held[at] for at in pair]
        if earlier:
            operands = after(operands, *earlier)
        fixed = (table, place, operands)
        part = tile if len(sides) == 2 else tile // 2
        if sides == (0,):
            (output,) = attend(sides, h, half, 0, part, tile, *fixed, [output], [width])
        elif sides == (1,):
            (passed,) = attend(sides, h, half, h, part, tile, *fixed, [passed], [hw])
        else:
            output, passed = attend(
                sides, h, half, h, part, tile, *fixed, [output, passed], [width, hw]
            )

    for i in range(len(order)):
        going = crossed[i]
        if i >= 2:
            last = i == len(order) - 1
            going = after(going, came[i - (3 if last else 2)])
        if i >= 4 and i % 2 == 0:
            going = after(going, output)
        came.append(move(going, onward))
        if i >= 3 and i % 2 == 1:
            compute((0, 1), (i - 3) // 2, crossed[i])
    compute((1,), half - 1)
    compute((0,), half - 1)

    back = move(passed, mates)

    def finish(core_ref, back_ref, _, out_ref, held, sems):
        column = lanes((1 - core_ref[0]) * hw, hw)
        for i, pair in enumerate([(back_ref, held), (held, out_ref.at[:, column])]):
            for copy in run_copies([pair], sems.at[pl.ds(i, 1)]):
                copy.wait()

    anywhere = pl.BlockSpec(memory_space=pl.ANY)
    return pl.pallas_call(
        finish,
        out_shape=jax.ShapeDtypeStruct((rows, width), queries.dtype),
        in_specs=[pl.BlockSpec(memory_space=pltpu.SMEM), anywhere, HBM],
        out_specs=HBM,
        scratch_shapes=[pltpu.VMEM((rows, hw), queries.dtype), pltpu.SemaphoreType.DMA((2,))],
        input_output_aliases={2: 0},
        compiler_params=pltpu.CompilerParams(vmem_limit_bytes=8 * 2**20),
    )(core_id, back, output)


def solution(mesh):
    spec = P(("groups", "blk"), None)
    return jax.shard_map(
        on_device, mesh=mesh, in_specs=(spec,) * 4, out_specs=spec, check_vma=False
    )
```

```python
import functools

import jax
import jax.numpy as jnp
from jax import lax
from jax.experimental import pallas as pl
from jax.experimental.pallas import tpu as pltpu
from jax.sharding import PartitionSpec as P

HD = 128
LOG2E = 1.4426950408889634
EARLY = 3
VMEM_BYTES = 56 * 2**20
SOURCES = 6
SMALL = pl.CostEstimate(flops=1, bytes_accessed=1, transcendentals=0)
HBM = pl.BlockSpec(memory_space=pltpu.HBM)


def lanes(start, size):
    return pl.ds(pl.multiple_of(start, HD), size)


def run_copies(pairs, sems):
    made = [pltpu.make_async_copy(a, b, sems.at[i]) for i, (a, b) in enumerate(pairs)]
    for copy in made:
        copy.start()
    return made


def pack(plan, core, operands, shapes, most):
    count = len(operands)
    made = len(shapes)
    kind = operands[0].dtype

    def body(core_ref, *refs):
        outs = refs[count : count + made]
        held = refs[count + made : -2]
        in_sems, out_sems = refs[-2:]
        loads = [
            run_copies(pairs, in_sems.at[i])
            for i, pairs in enumerate(plan(core_ref[0], refs[:count], held))
        ]
        stores = []
        for i, load in enumerate(loads):
            for copy in load:
                copy.wait()
            stores += run_copies([(held[i], outs[i])], out_sems.at[pl.ds(i, 1)])
        for copy in stores:
            copy.wait()

    return pl.pallas_call(
        body,
        out_shape=[jax.ShapeDtypeStruct(shape, kind) for shape in shapes],
        in_specs=[pl.BlockSpec(memory_space=pltpu.SMEM)] + [HBM] * count,
        out_specs=[HBM] * made,
        scratch_shapes=[pltpu.VMEM(shape, kind) for shape in shapes]
        + [pltpu.SemaphoreType.DMA((made, most)), pltpu.SemaphoreType.DMA((made,))],
        compiler_params=pltpu.CompilerParams(vmem_limit_bytes=VMEM_BYTES),
        cost_estimate=SMALL,
    )(core, *operands)


def head_kernel(sides, head, half, to_col, slots, tile, table, place, *refs):
    queries, m_q = refs[:2]
    blocks = refs[2 : 2 + SOURCES]
    outs = refs[-8 - len(sides) : -8]
    q_win, k_win, v_win, o_win, s_even, s_odd, sems, out_sems = refs[-8:]
    rows = queries.shape[0]
    col = lanes((place[SOURCES] * half + head) * HD, HD)
    q_from = (queries.at[:, col], m_q.at[:, pl.ds(head * HD, HD)])
    where = [pl.ds(pl.multiple_of(place[s] * rows, rows), rows) for s in range(SOURCES)]
    loads = [(q_from[side], q_win.at[pl.ds(i * rows, rows)]) for i, side in enumerate(sides)]
    for i, window in enumerate((k_win, v_win)):
        for s, block in enumerate(blocks):
            at = pl.ds((2 * head + i if s == 1 else i) * rows, rows)
            loads.append((block.at[at], window.at[where[s]]))
    loads = run_copies(loads, sems)
    for copy in loads[:-SOURCES]:
        copy.wait()

    factor = HD**-0.5 * LOG2E
    scores = (s_even, s_odd)
    part = s_even.shape[1]
    tiles = rows // tile
    units = [(t, r) for t in range(len(sides) * tiles) for r in range(0, tile, part)]
    peaks = {}
    stores = []

    def named(t, j):
        at = table[(sides[t // tiles] * tiles + t % tiles) * slots + j]
        return at >= 0, pl.ds(pl.multiple_of(jnp.maximum(at, 0) * tile, tile), tile)

    for u in range(len(units) + 1):
        peak = total = summed = None
        if u == 1:
            for copy in loads[-SOURCES:]:
                copy.wait()
        for j in range(slots):
            if u < len(units):
                t, r = units[u]
                valid, at = named(t, j)
                s = lax.dot_general(
                    q_win[t * tile + r : t * tile + r + part, :],
                    k_win[at, :],
                    (((1,), (1,)), ((), ())),
                    preferred_element_type=jnp.float32,
                )
                s = s * factor
                scores[u % 2][j] = s
                most = s[:, :HD]
                for lane in range(HD, tile, HD):
                    most = jnp.maximum(most, s[:, lane : lane + HD])
                most = jnp.where(valid, most, -3e38)
                peak = most if peak is None else jnp.maximum(peak, most)
            if u > 0:
                valid, at = named(units[u - 1][0], j)
                above = jnp.where(valid, peaks[u - 1], 3e38)
                weights = jnp.exp2(scores[(u - 1) % 2][j] - above)
                added = weights[:, :HD]
                for lane in range(HD, tile, HD):
                    added = added + weights[:, lane : lane + HD]
                total = added if total is None else total + added
                term = jnp.dot(
                    weights.astype(jnp.bfloat16),
                    v_win[at, :],
                    preferred_element_type=jnp.float32,
                )
                summed = term if summed is None else summed + term
        if u < len(units):
            peaks[u] = jnp.max(peak, axis=1, keepdims=True)
        if u > 0:
            t, r = units[u - 1]
            result = summed / jnp.sum(total, axis=1, keepdims=True)
            o_win[t * tile + r : t * tile + r + part, :] = result.astype(o_win.dtype)
            if t % tiles == tiles - 1 and r + part == tile:
                i = t // tiles
                to = col if sides[i] == 0 else pl.ds(to_col * HD, HD)
                pair = (o_win.at[pl.ds(i * rows, rows)], outs[i].at[:, to])
                stores += run_copies([pair], out_sems.at[pl.ds(i, 1)])
    for copy in stores:
        copy.wait()


def attend(sides, head, half, to_col, part, tile, table, place, operands, previous, widths):
    rows = operands[0].shape[0]
    slots = table.shape[0] // (2 * (rows // tile))
    kind = operands[0].dtype
    smem = pl.BlockSpec(memory_space=pltpu.SMEM)
    ins = [table, place, *operands]
    aliases = {}
    for i, array in enumerate(previous):
        if array is not None:
            aliases[len(ins)] = i
            ins.append(array)
    count = len(sides)
    return pl.pallas_call(
        functools.partial(head_kernel, sides, head, half, to_col, slots, tile),
        out_shape=[jax.ShapeDtypeStruct((rows, width), kind) for width in widths],
        in_specs=[smem] * 2 + [HBM] * (len(ins) - 2),
        out_specs=[HBM] * count,
        scratch_shapes=[
            pltpu.VMEM((count * rows, HD), kind),
            pltpu.VMEM((SOURCES * rows, HD), kind),
            pltpu.VMEM((SOURCES * rows, HD), kind),
            pltpu.VMEM((count * rows, HD), kind),
            pltpu.VMEM((slots, part, tile), jnp.float32),
            pltpu.VMEM((slots, part, tile), jnp.float32),
            pltpu.SemaphoreType.DMA((count + 2 * SOURCES,)),
            pltpu.SemaphoreType.DMA((count,)),
        ],
        input_output_aliases=aliases,
        compiler_params=pltpu.CompilerParams(vmem_limit_bytes=VMEM_BYTES),
        cost_estimate=SMALL,
    )(*ins)


def on_device(queries, keys, values, neighbours):
    rows, width = queries.shape
    tiles = neighbours.shape[0]
    tile = rows // tiles
    count = lax.axis_size("blk")
    block = lax.axis_index("blk")
    half = width // HD // 2
    hw = half * HD
    core = lax.rem(block, 2)
    upper = lax.rem(block // 2, 2)

    mates = [(b, b ^ 1) for b in range(count)]
    across = [(b, b ^ 2) for b in range(count)]
    onward = [(b, (b + 4 if b % 4 < 2 else b - 4) % count) for b in range(count)]

    def move(value, pairs):
        return lax.ppermute(value, "blk", pairs)

    crossed_at = 4 * (1 - upper)
    place = jnp.stack(
        [
            2 + core,
            3 - core,
            crossed_at + core,
            crossed_at + 1 - core,
            4 - crossed_at + core,
            5 - crossed_at - core,
            core,
        ]
    ).astype(jnp.int32)
    core_id = core.astype(jnp.int32).reshape(1)


    def cut(refs, head, out):
        col = lanes(head * HD, HD)
        return [(refs[i].at[:, col], out.at[pl.ds(i * rows, rows)]) for i in range(2)]

    def plan_first(k, refs, outs):
        plans = [cut(refs, k * half + h, outs[h]) for h in range(EARLY)]
        away = []
        for h in range(half):
            to = outs[EARLY].at[pl.ds(2 * h * rows, 2 * rows)]
            away += cut(refs, (1 - k) * half + h, to)
        return plans + [away]

    def plan_second(k, refs, outs):
        plans = [cut(refs, k * half + h, outs[h - EARLY]) for h in range(EARLY, half)]
        return plans + [[(refs[2].at[:, lanes((1 - k) * hw, hw)], outs[-1])]]

    def after(value, *earlier):
        return lax.optimization_barrier((value, earlier))[0]

    piece = (2 * rows, HD)
    crossed = []
    *own, kv_away = pack(
        plan_first, core_id, (keys, values), [piece] * EARLY + [(2 * half * rows, HD)], 2 * half
    )
    m_kv = move(kv_away, mates)
    crossed.append(move(own[0], across))
    *rest, q_away = pack(
        plan_second,
        core_id,
        (keys, values, queries),
        [piece] * (half - EARLY) + [(rows, hw)],
        2,
    )
    own += rest
    m_q = move(q_away, mates)
    base = (block - core - 2) * tiles
    listed = jnp.concatenate([neighbours, move(neighbours, mates)], axis=0)
    table = jnp.where(listed >= 0, listed - base, -1).reshape(-1).astype(jnp.int32)
    order = [(0, 0), (0, 1), (1, 0), (1, 1)]
    order += [(side, h) for h in range(2, half) for side in (0, 1)]
    for i, entry in enumerate(order):
        if i == 0:
            continue
        side, h = entry
        going = m_kv[2 * h * rows : 2 * (h + 1) * rows] if side else own[h]
        lag = 2 if i < 5 else 4
        if i >= lag:
            going = after(going, crossed[i - lag])
        crossed.append(move(going, across))

    spot = {entry: i for i, entry in enumerate(order)}
    came = []
    output = None
    passed = None

    def compute(sides, h, *earlier):
        nonlocal output, passed
        pair = [spot[(0, h)], spot[(1, h)]]
        operands = [queries, m_q, own[h], m_kv]
        for held in (crossed, came):
            operands += [held[at] for at in pair]
        if earlier:
            operands = after(operands, *earlier)
        fixed = (table, place, operands)
        part = tile if len(sides) == 2 else tile // 2
        if sides == (0,):
            (output,) = attend(sides, h, half, 0, part, tile, *fixed, [output], [width])
        elif sides == (1,):
            (passed,) = attend(sides, h, half, h, part, tile, *fixed, [passed], [hw])
        else:
            output, passed = attend(
                sides, h, half, h, part, tile, *fixed, [output, passed], [width, hw]
            )

    for i in range(len(order)):
        going = crossed[i]
        if i >= 2:
            last = i == len(order) - 1
            going = after(going, came[i - (3 if last else 2)])
        if i >= 4 and i % 2 == 0:
            going = after(going, output)
        came.append(move(going, onward))
        if i >= 3 and i % 2 == 1:
            compute((0, 1), (i - 3) // 2, crossed[i])
    compute((0, 1), half - 1)

    back = move(passed, mates)

    def finish(core_ref, back_ref, _, out_ref, held, sems):
        column = lanes((1 - core_ref[0]) * hw, hw)
        for i, pair in enumerate([(back_ref, held), (held, out_ref.at[:, column])]):
            for copy in run_copies([pair], sems.at[pl.ds(i, 1)]):
                copy.wait()

    anywhere = pl.BlockSpec(memory_space=pl.ANY)
    return pl.pallas_call(
        finish,
        out_shape=jax.ShapeDtypeStruct((rows, width), queries.dtype),
        in_specs=[pl.BlockSpec(memory_space=pltpu.SMEM), anywhere, HBM],
        out_specs=HBM,
        scratch_shapes=[pltpu.VMEM((rows, hw), queries.dtype), pltpu.SemaphoreType.DMA((2,))],
        input_output_aliases={2: 0},
        compiler_params=pltpu.CompilerParams(vmem_limit_bytes=8 * 2**20),
    )(core_id, back, output)


def solution(mesh):
    spec = P(("groups", "blk"), None)
    return jax.shard_map(
        on_device, mesh=mesh, in_specs=(spec,) * 4, out_specs=spec, check_vma=False
    )
```

```python
import functools

import jax
import jax.numpy as jnp
from jax import lax
from jax.experimental import pallas as pl
from jax.experimental.pallas import tpu as pltpu
from jax.sharding import PartitionSpec as P

HD = 128
LOG2E = 1.4426950408889634
EARLY = 2
VMEM_BYTES = 63 * 2**20
SOURCES = 6
SMALL = pl.CostEstimate(flops=1, bytes_accessed=1, transcendentals=0)
HBM = pl.BlockSpec(memory_space=pltpu.HBM)


def lanes(start, size):
    return pl.ds(pl.multiple_of(start, HD), size)


def run_copies(pairs, sems):
    made = [pltpu.make_async_copy(a, b, sems.at[i]) for i, (a, b) in enumerate(pairs)]
    for copy in made:
        copy.start()
    return made


def pack(plan, core, operands, shapes, most):
    count = len(operands)
    made = len(shapes)
    kind = operands[0].dtype

    def body(core_ref, *refs):
        outs = refs[count : count + made]
        held = refs[count + made : -2]
        in_sems, out_sems = refs[-2:]
        loads = [
            run_copies(pairs, in_sems.at[i])
            for i, pairs in enumerate(plan(core_ref[0], refs[:count], held))
        ]
        stores = []
        for i, load in enumerate(loads):
            for copy in load:
                copy.wait()
            stores += run_copies([(held[i], outs[i])], out_sems.at[pl.ds(i, 1)])
        for copy in stores:
            copy.wait()

    return pl.pallas_call(
        body,
        out_shape=[jax.ShapeDtypeStruct(shape, kind) for shape in shapes],
        in_specs=[pl.BlockSpec(memory_space=pltpu.SMEM)] + [HBM] * count,
        out_specs=[HBM] * made,
        scratch_shapes=[pltpu.VMEM(shape, kind) for shape in shapes]
        + [pltpu.SemaphoreType.DMA((made, most)), pltpu.SemaphoreType.DMA((made,))],
        compiler_params=pltpu.CompilerParams(vmem_limit_bytes=VMEM_BYTES),
        cost_estimate=SMALL,
    )(core, *operands)


def head_kernel(sides, head, half, to_col, slots, tile, table, place, *refs):
    queries, m_q = refs[:2]
    blocks = refs[2 : 2 + SOURCES]
    outs = refs[-8 - len(sides) : -8]
    q_win, k_win, v_win, o_win, s_even, s_odd, sems, out_sems = refs[-8:]
    rows = queries.shape[0]
    col = lanes((place[SOURCES] * half + head) * HD, HD)
    q_from = (queries.at[:, col], m_q.at[:, pl.ds(head * HD, HD)])
    where = [pl.ds(pl.multiple_of(place[s] * rows, rows), rows) for s in range(SOURCES)]
    loads = [(q_from[side], q_win.at[pl.ds(i * rows, rows)]) for i, side in enumerate(sides)]
    for i, window in enumerate((k_win, v_win)):
        for s, block in enumerate(blocks):
            at = pl.ds((2 * head + i if s == 1 else i) * rows, rows)
            loads.append((block.at[at], window.at[where[s]]))
    loads = run_copies(loads, sems)
    for copy in loads[:-SOURCES]:
        copy.wait()

    factor = HD**-0.5 * LOG2E
    scores = (s_even, s_odd)
    part = s_even.shape[1]
    tiles = rows // tile
    units = [(t, r) for t in range(len(sides) * tiles) for r in range(0, tile, part)]
    peaks = {}
    stores = []

    def named(t, j):
        at = table[(sides[t // tiles] * tiles + t % tiles) * slots + j]
        return at >= 0, pl.ds(pl.multiple_of(jnp.maximum(at, 0) * tile, tile), tile)

    for u in range(len(units) + 1):
        peak = total = summed = None
        if u == 1:
            for copy in loads[-SOURCES:]:
                copy.wait()
        for j in range(slots):
            if u < len(units):
                t, r = units[u]
                valid, at = named(t, j)
                s = lax.dot_general(
                    q_win[t * tile + r : t * tile + r + part, :],
                    k_win[at, :],
                    (((1,), (1,)), ((), ())),
                    preferred_element_type=jnp.float32,
                )
                s = s * factor
                scores[u % 2][j] = s
                most = s[:, :HD]
                for lane in range(HD, tile, HD):
                    most = jnp.maximum(most, s[:, lane : lane + HD])
                most = jnp.where(valid, most, -3e38)
                peak = most if peak is None else jnp.maximum(peak, most)
            if u > 0:
                valid, at = named(units[u - 1][0], j)
                above = jnp.where(valid, peaks[u - 1], 3e38)
                weights = jnp.exp2(scores[(u - 1) % 2][j] - above)
                added = weights[:, :HD]
                for lane in range(HD, tile, HD):
                    added = added + weights[:, lane : lane + HD]
                total = added if total is None else total + added
                term = jnp.dot(
                    weights.astype(jnp.bfloat16),
                    v_win[at, :],
                    preferred_element_type=jnp.float32,
                )
                summed = term if summed is None else summed + term
        if u < len(units):
            peaks[u] = jnp.max(peak, axis=1, keepdims=True)
        if u > 0:
            t, r = units[u - 1]
            result = summed / jnp.sum(total, axis=1, keepdims=True)
            o_win[t * tile + r : t * tile + r + part, :] = result.astype(o_win.dtype)
            if t % tiles == tiles - 1 and r + part == tile:
                i = t // tiles
                to = col if sides[i] == 0 else pl.ds(to_col * HD, HD)
                pair = (o_win.at[pl.ds(i * rows, rows)], outs[i].at[:, to])
                stores += run_copies([pair], out_sems.at[pl.ds(i, 1)])
    for copy in stores:
        copy.wait()


def attend(sides, head, half, to_col, part, tile, table, place, operands, previous, widths):
    rows = operands[0].shape[0]
    slots = table.shape[0] // (2 * (rows // tile))
    kind = operands[0].dtype
    smem = pl.BlockSpec(memory_space=pltpu.SMEM)
    ins = [table, place, *operands]
    aliases = {}
    for i, array in enumerate(previous):
        if array is not None:
            aliases[len(ins)] = i
            ins.append(array)
    count = len(sides)
    return pl.pallas_call(
        functools.partial(head_kernel, sides, head, half, to_col, slots, tile),
        out_shape=[jax.ShapeDtypeStruct((rows, width), kind) for width in widths],
        in_specs=[smem] * 2 + [HBM] * (len(ins) - 2),
        out_specs=[HBM] * count,
        scratch_shapes=[
            pltpu.VMEM((count * rows, HD), kind),
            pltpu.VMEM((SOURCES * rows, HD), kind),
            pltpu.VMEM((SOURCES * rows, HD), kind),
            pltpu.VMEM((count * rows, HD), kind),
            pltpu.VMEM((slots, part, tile), jnp.float32),
            pltpu.VMEM((slots, part, tile), jnp.float32),
            pltpu.SemaphoreType.DMA((count + 2 * SOURCES,)),
            pltpu.SemaphoreType.DMA((count,)),
        ],
        input_output_aliases=aliases,
        compiler_params=pltpu.CompilerParams(vmem_limit_bytes=VMEM_BYTES),
        cost_estimate=SMALL,
    )(*ins)


def on_device(queries, keys, values, neighbours):
    rows, width = queries.shape
    tiles = neighbours.shape[0]
    tile = rows // tiles
    count = lax.axis_size("blk")
    block = lax.axis_index("blk")
    half = width // HD // 2
    hw = half * HD
    core = lax.rem(block, 2)
    upper = lax.rem(block // 2, 2)

    mates = [(b, b ^ 1) for b in range(count)]
    across = [(b, b ^ 2) for b in range(count)]
    onward = [(b, (b + 4 if b % 4 < 2 else b - 4) % count) for b in range(count)]

    def move(value, pairs):
        return lax.ppermute(value, "blk", pairs)

    crossed_at = 4 * (1 - upper)
    place = jnp.stack(
        [
            2 + core,
            3 - core,
            crossed_at + core,
            crossed_at + 1 - core,
            4 - crossed_at + core,
            5 - crossed_at - core,
            core,
        ]
    ).astype(jnp.int32)
    core_id = core.astype(jnp.int32).reshape(1)


    def cut(refs, head, out):
        col = lanes(head * HD, HD)
        return [(refs[i].at[:, col], out.at[pl.ds(i * rows, rows)]) for i in range(2)]

    def plan_first(k, refs, outs):
        plans = [cut(refs, k * half + h, outs[h]) for h in range(EARLY)]
        away = []
        for h in range(half):
            to = outs[EARLY].at[pl.ds(2 * h * rows, 2 * rows)]
            away += cut(refs, (1 - k) * half + h, to)
        return plans + [away]

    def plan_second(k, refs, outs):
        plans = [cut(refs, k * half + h, outs[h - EARLY]) for h in range(EARLY, half)]
        return plans + [[(refs[2].at[:, lanes((1 - k) * hw, hw)], outs[-1])]]

    def after(value, *earlier):
        return lax.optimization_barrier((value, earlier))[0]

    piece = (2 * rows, HD)
    crossed = []
    *own, kv_away = pack(
        plan_first, core_id, (keys, values), [piece] * EARLY + [(2 * half * rows, HD)], 2 * half
    )
    m_kv = move(kv_away, mates)
    crossed.append(move(own[0], across))
    *rest, q_away = pack(
        plan_second,
        core_id,
        (keys, values, queries),
        [piece] * (half - EARLY) + [(rows, hw)],
        2,
    )
    own += rest
    m_q = move(q_away, mates)
    base = (block - core - 2) * tiles
    listed = jnp.concatenate([neighbours, move(neighbours, mates)], axis=0)
    table = jnp.where(listed >= 0, listed - base, -1).reshape(-1).astype(jnp.int32)
    order = [(0, 0), (0, 1), (1, 0), (1, 1)]
    order += [(side, h) for h in range(2, half) for side in (0, 1)]
    for i, entry in enumerate(order):
        if i == 0:
            continue
        side, h = entry
        going = m_kv[2 * h * rows : 2 * (h + 1) * rows] if side else own[h]
        lag = 2 if i < 5 else 4
        if i >= lag:
            going = after(going, crossed[i - lag])
        crossed.append(move(going, across))

    spot = {entry: i for i, entry in enumerate(order)}
    came = []
    output = None
    passed = None

    def compute(sides, h, *earlier):
        nonlocal output, passed
        pair = [spot[(0, h)], spot[(1, h)]]
        operands = [queries, m_q, own[h], m_kv]
        for held in (crossed, came):
            operands += [held[at] for at in pair]
        if earlier:
            operands = after(operands, *earlier)
        fixed = (table, place, operands)
        part = tile if len(sides) == 2 else tile // 2
        if sides == (0,):
            (output,) = attend(sides, h, half, 0, part, tile, *fixed, [output], [width])
        elif sides == (1,):
            (passed,) = attend(sides, h, half, h, part, tile, *fixed, [passed], [hw])
        else:
            output, passed = attend(
                sides, h, half, h, part, tile, *fixed, [output, passed], [width, hw]
            )

    for i in range(len(order)):
        going = crossed[i]
        if i >= 2:
            last = i == len(order) - 1
            going = after(going, came[i - (3 if last else 2)])
        if i >= 4 and i % 2 == 0:
            going = after(going, output)
        came.append(move(going, onward))
        if i >= 3 and i % 2 == 1:
            compute((0, 1), (i - 3) // 2, crossed[i])
    compute((0, 1), half - 1)

    back = move(passed, mates)

    def finish(core_ref, back_ref, _, out_ref, held, sems):
        column = lanes((1 - core_ref[0]) * hw, hw)
        for i, pair in enumerate([(back_ref, held), (held, out_ref.at[:, column])]):
            for copy in run_copies([pair], sems.at[pl.ds(i, 1)]):
                copy.wait()

    anywhere = pl.BlockSpec(memory_space=pl.ANY)
    return pl.pallas_call(
        finish,
        out_shape=jax.ShapeDtypeStruct((rows, width), queries.dtype),
        in_specs=[pl.BlockSpec(memory_space=pltpu.SMEM), anywhere, HBM],
        out_specs=HBM,
        scratch_shapes=[pltpu.VMEM((rows, hw), queries.dtype), pltpu.SemaphoreType.DMA((2,))],
        input_output_aliases={2: 0},
        compiler_params=pltpu.CompilerParams(vmem_limit_bytes=8 * 2**20),
    )(core_id, back, output)


def solution(mesh):
    spec = P(("groups", "blk"), None)
    return jax.shard_map(
        on_device, mesh=mesh, in_specs=(spec,) * 4, out_specs=spec, check_vma=False
    )
```
